32 devices in a mesh: section: 2 (over core), dp: 16 (over z, y, x).
Axes of the slice: x: 2, y: 2, z: 4, core: 2. Of those that a mesh axis runs over, the one named last changes fastest.
Arguments:
- tokens: bfloat16 [2, 8192, 768], P(None, 'dp'), may hold values from -36 to 36, as said below
- segment_ids: int32 [2, 8192], P(None, 'dp'), may hold values from -1 to 15, as said below
- w_qkv: bfloat16 [2, 768, 2304], P('section'), may hold values from -0.21875 to 0.21875
- w_attn_out: bfloat16 [2, 768, 768], P('section'), may hold values from -0.875 to 0.875
- w_ff_in: bfloat16 [2, 768, 3072], P('section'), may hold values from -0.21875 to 0.21875
- w_ff_out: bfloat16 [2, 3072, 768], P('section'), may hold values from -0.109375 to 0.109375
- adapter_down: bfloat16 [2, 2, 768, 64], P('section'), may hold values from -0.21875 to 0.21875
- adapter_down_bias: float32 [2, 2, 64], P('section'), may hold values from -3 to 3
- adapter_up: bfloat16 [2, 2, 64, 768], P('section'), may hold values from -0.75 to 0.75
- adapter_up_bias: float32 [2, 2, 768], P('section'), may hold values from -3 to 3
- ln_gain: float32 [2, 2, 768], P('section'), may hold values from 0.5 to 1.5
- ln_bias: float32 [2, 2, 768], P('section'), may hold values from -2 to 2
- cotangent: bfloat16 [2, 8192, 768], P(None, 'dp'), may hold values from -6 to 6
Outputs:
- layer_outputs: bfloat16 [2, 2, 8192, 768], P('section', None, 'dp')
- input_grads: float32 [2, 2, 8192, 768], P('section', None, 'dp')
- grad_adapter_down: float32 [2, 2, 768, 64], P('section')
- grad_adapter_down_bias: float32 [2, 2, 64], P('section')
- grad_adapter_up: float32 [2, 2, 64, 768], P('section')
- grad_adapter_up_bias: float32 [2, 2, 768], P('section')
- grad_ln_gain: float32 [2, 2, 768], P('section')
- grad_ln_bias: float32 [2, 2, 768], P('section')
- rms_stats: float32 [2, 3], P('section')
The draws below stay inside these ranges and needn't reach their ends.
Inputs may be any that keep to these rules, and one draw needn't show every extreme that they name: `segment_ids`: in each micro-batch each aligned block of 512 slots holds either one item of 384 tokens (id 0) in its first slots, or items of 32 tokens numbered 0, 1, 2, ... in order, then any padding (-1); items never cross blocks, and every block has a valid token. Blocks 2p and 2p + 1 together hold at most 768 valid tokens, and some pair holds exactly that. `tokens`: Real-valued activations of order one.
All inputs are finite; a program needn't handle non-finite values.
Results may differ from the reference program's by a relative error of at most 0.025.
Values may be sent and summed in bfloat16 or wider, within the bound.
No kernel may reach another device: no remote copies, remote signals or barrier semaphores. Data moves between devices by JAX's collectives and lax.ppermute only.
A program may use at most 256 MiB of HBM per device.

```python
from functools import partial
import jax
import jax.numpy as jnp
from jax import lax

D = 768
HEADS = 12
HEAD_DIM = 64
FF = 3072
ADAPT = 64
MB = 2
ROWS = 512
SHORT = 32
CAP = 384
TOKENS = 8192


def draw_tokens(key, part):
    key = jax.random.fold_in(key, 11)
    devices = TOKENS // ROWS
    place = (jnp.arange(TOKENS) // ROWS).astype(jnp.float32) / (devices - 1)
    scale = 1.0 + 2.0 * place
    noise = jnp.clip(jax.random.normal(key, (MB, TOKENS, D), jnp.float32), -6.0, 6.0)
    return (noise * scale[None, :, None]).astype(jnp.bfloat16)


def draw_segment_ids(key, part):
    key = jax.random.fold_in(key, 7)
    devices = TOKENS // ROWS
    pairs = devices // 2
    item_count = ROWS // SHORT
    pair_items = 2 * (CAP // SHORT)
    long_items = CAP // SHORT
    limit = pair_items - item_count
    key_jitter, key_long, key_side, key_pick = jax.random.split(key, 4)
    positions = jnp.arange(devices)
    base_count = 1 + (item_count - 1) * positions // (devices - 1)
    jitter = jax.random.randint(key_jitter, (MB, devices), -2, 3)
    counts = jnp.clip(base_count[None, :] + jitter, 1, item_count).reshape(MB, pairs, 2)
    even = counts[:, :, 0]
    odd = jnp.minimum(counts[:, :, 1], pair_items - even)
    long_pair = jax.random.randint(key_long, (MB, pairs), 0, 4) == 0
    side = jax.random.randint(key_side, (MB, pairs), 0, 2)
    picked = jax.random.randint(key_pick, (), 1, pairs - 1)
    long_pair = long_pair.at[0, picked].set(True).at[0, 0].set(False).at[0, pairs - 1].set(False)
    long_even = long_pair & (side == 0)
    long_odd = long_pair & (side == 1)
    even = jnp.where(long_odd, jnp.minimum(even, long_items), even)
    odd = jnp.where(long_even, jnp.minimum(odd, long_items), odd)
    even = even.at[0, 0].set(1).at[0, pairs - 1].set(limit)
    odd = odd.at[0, pairs - 1].set(item_count)
    counts = jnp.stack([even, odd], -1).reshape(MB, devices)
    chosen = jnp.stack([long_even, long_odd], -1).reshape(MB, devices)
    slot_index = jnp.arange(ROWS)
    slot_item = slot_index // SHORT
    item_ids = jnp.where(slot_item[None, None, :] < counts[:, :, None], slot_item[None, None, :], -1)
    long_ids = jnp.where(slot_index < CAP, 0, -1)
    item_ids = jnp.where(chosen[:, :, None], long_ids[None, None, :], item_ids)
    return item_ids.reshape(MB, TOKENS).astype(jnp.int32)


def steps_of(rng, dims, cuts, least, largest):
    level, own = 1.0, jax.random.fold_in(rng, 6)
    for dim, blocks in cuts:
        steps = jnp.exp(jax.random.uniform(jax.random.fold_in(own, dim), (blocks,), jnp.float32, least / len(cuts), largest / len(cuts)))
        level = level * jnp.repeat(steps, dims[dim] // blocks).reshape([-1 if axis == dim else 1 for axis in range(len(dims))])
    return level


def centred(stream_key, extent, width, most, cuts=(), kind=jnp.bfloat16):
    values = width * jax.random.normal(stream_key, extent, jnp.float32)
    if cuts:
        values = values * steps_of(stream_key, extent, cuts, -0.22, 0.18)
    return jnp.clip(values, -most, most).astype(kind)


def setup_inputs(seed: int = 0) -> dict:
    splits = jax.random.split(jax.random.key(seed), 14)
    tokens = draw_tokens(jax.random.fold_in(splits[13], 71), 0)
    segment_ids = draw_segment_ids(jax.random.fold_in(splits[13], 71), 0)
    w_qkv = centred(splits[2], (2, D, 3 * D), D ** -0.5, 0.21875, ((0, 2),))
    w_attn_out = centred(splits[3], (2, D, D), (D // 16) ** -0.5, 0.875, ((0, 2),))
    w_ff_in = centred(splits[4], (2, D, FF), D ** -0.5, 0.21875, ((0, 2),))
    w_ff_out = centred(splits[5], (2, FF, D), FF ** -0.5, 0.109375, ((0, 2),))
    adapter_down = centred(splits[6], (2, 2, D, ADAPT), D ** -0.5, 0.21875, ((0, 2),))
    adapter_down_bias = centred(splits[7], (2, 2, ADAPT), 0.5, 3.0, ((0, 2),), jnp.float32)
    adapter_up = centred(splits[8], (2, 2, ADAPT, D), ADAPT ** -0.5, 0.75, ((0, 2),))
    adapter_up_bias = centred(splits[9], (2, 2, D), 0.5, 3.0, ((0, 2),), jnp.float32)
    ln_gain = jnp.clip(1.0 + 0.1 * jax.random.normal(splits[10], (2, 2, D), jnp.float32), 0.5, 1.5)
    ln_bias = centred(splits[11], (2, 2, D), 0.3, 2.0, ((0, 2),), jnp.float32)
    cotangent = centred(splits[12], (MB, TOKENS, D), 1.0, 6.0, ((1, 16),))
    return {"tokens": tokens, "segment_ids": segment_ids, "w_qkv": w_qkv, "w_attn_out": w_attn_out, "w_ff_in": w_ff_in, "w_ff_out": w_ff_out, "adapter_down": adapter_down, "adapter_down_bias": adapter_down_bias, "adapter_up": adapter_up, "adapter_up_bias": adapter_up_bias, "ln_gain": ln_gain, "ln_bias": ln_bias, "cotangent": cotangent}


@jax.custom_vjp
def low(v):
    return lax.optimization_barrier(v.astype(jnp.bfloat16)).astype(jnp.float32)

@jax.custom_vjp
def low_back(v):
    return v

def low_keep(v):
    return (low(v), None)

def low_pass(kept, grad):
    return (grad,)

def back_keep(v):
    return (v, None)

def back_low(kept, grad):
    return (low(grad),)
low.defvjp(low_keep, low_pass)
low_back.defvjp(back_keep, back_low)

def product(left, right):
    return jnp.dot(left, right, precision=lax.Precision.HIGHEST, preferred_element_type=jnp.float32)

def gelu_exact(values):
    return jax.nn.gelu(values, approximate=False)

def layer_norm(values, gain, shift):
    centre = values - lax.optimization_barrier(jnp.mean(values, -1, keepdims=True))
    spread = lax.optimization_barrier(jnp.mean(centre * centre, -1, keepdims=True))
    return centre * lax.rsqrt(spread + 1e-05) * gain + shift

def attend_block(pair):
    united, labels = pair
    length = united.shape[0]
    queries = united[:, :D].reshape(length, HEADS, HEAD_DIM)
    keys_all = united[:, D:2 * D].reshape(length, HEADS, HEAD_DIM)
    values = united[:, 2 * D:].reshape(length, HEADS, HEAD_DIM)
    raw = jnp.einsum('qhd,khd->hqk', queries, keys_all, precision=lax.Precision.HIGHEST) * HEAD_DIM ** (-0.5)
    allowed = (labels[:, None] == labels[None, :])[None]
    scores = jnp.where(allowed, low_back(raw), -1e+30)
    highest = lax.optimization_barrier(jnp.max(scores, -1, keepdims=True))
    exponent = jnp.exp(scores - highest)
    attention = exponent / lax.optimization_barrier(jnp.sum(exponent, -1, keepdims=True))
    merged = jnp.einsum('hqk,khd->qhd', low(attention), values, precision=lax.Precision.HIGHEST).reshape(length, D)
    return low_back(low(merged))

def adapter(source, down, down_bias, up, up_bias):
    before = low_back(product(low(source), down) + down_bias)
    return low_back(product(low(gelu_exact(before)), up) + up_bias)

def layer_pass(inputs, down, down_bias, up, up_bias, gain, shift, frozen, blocks, valid_rows):
    w_united, w_out, w_in, w_back = frozen
    row_weight = valid_rows[:, None]
    united = low_back(low(product(inputs, w_united)))
    merged = lax.map(jax.checkpoint(attend_block), (united.reshape(-1, ROWS, 3 * D), blocks)).reshape(-1, D)
    attended = low_back(product(merged, w_out))
    branch_one = attended + adapter(attended, down[0], down_bias[0], up[0], up_bias[0])
    normed = layer_norm(inputs + branch_one, gain[0], shift[0])
    hidden = low_back(product(low(normed), w_in))
    expanded = low_back(product(low(gelu_exact(hidden)), w_back))
    branch_two = expanded + adapter(expanded, down[1], down_bias[1], up[1], up_bias[1])
    result = layer_norm(normed + branch_two, gain[1], shift[1])
    totals = jnp.stack([jnp.sum(row_weight * inputs * inputs), jnp.sum(row_weight * branch_one * branch_one), jnp.sum(row_weight * branch_two * branch_two)])
    return (low_back(low(result * row_weight)), totals)

def reference(tokens, segment_ids, w_qkv, w_attn_out, w_ff_in, w_ff_out, adapter_down, adapter_down_bias, adapter_up, adapter_up_bias, ln_gain, ln_bias, cotangent):
    blocks = segment_ids.reshape(-1, ROWS)
    valid_rows = (segment_ids.reshape(-1) >= 0).astype(jnp.float32)

    def section_pass(level, inputs):
        frozen = tuple((weight_arg[level].astype(jnp.float32) for weight_arg in (w_qkv, w_attn_out, w_ff_in, w_ff_out)))
        layer_fn = partial(layer_pass, frozen=frozen, blocks=blocks, valid_rows=valid_rows)
        trained = tuple((weight_arg[level].astype(jnp.float32) for weight_arg in (adapter_down, adapter_down_bias, adapter_up, adapter_up_bias, ln_gain, ln_bias)))
        return jax.vjp(layer_fn, inputs, *trained, has_aux=True)
    first, back_first, stats_first = section_pass(0, tokens.astype(jnp.float32).reshape(-1, D))
    second, back_second, stats_second = section_pass(1, first)
    grads_second = back_second(cotangent.astype(jnp.float32).reshape(-1, D))
    grads_first = back_first(grads_second[0])
    shape_out = (2, MB, TOKENS, D)
    layer_outputs = jnp.stack([first, second]).reshape(shape_out).astype(jnp.bfloat16)
    input_grads = jnp.stack([grads_first[0], grads_second[0]]).reshape(shape_out)
    stacked = [jnp.stack([grads_first[entry], grads_second[entry]]) for entry in range(1, 7)]
    rms_stats = jnp.sqrt(jnp.stack([stats_first, stats_second]) / (jnp.sum(valid_rows) * D))
    return (layer_outputs, input_grads, stacked[0], stacked[1], stacked[2], stacked[3], stacked[4], stacked[5], rms_stats)
```

```python
from functools import partial
from itertools import chain
from types import SimpleNamespace

import jax
import jax.numpy as jnp
from jax import lax
from jax.experimental import pallas as pl
from jax.experimental.pallas import tpu as pltpu
from jax.sharding import PartitionSpec as P

HEADS = 12
ITEM = 32
UNIT = 256
TILE = 128
PAIR = 128
LOG2E = 1.4426950408889634
SCOPED = 10 * 2**20
BLOCK = 64
LONG_TOGETHER = 2
EARLY = 2
LN2 = 0.6931471805599453
bf16 = jnp.bfloat16
f32 = jnp.float32

ERF = (0.7977178338317933, 0.03679825608874024, -0.00031580706578781924)
PDF = 0.3989422804014327


def mm(left, right):
    return lax.dot_general(left, right, (((1,), (0,)), ((), ())), preferred_element_type=f32)


def mm_t(left, right):
    return lax.dot_general(left, right, (((1,), (1,)), ((), ())), preferred_element_type=f32)


def gelu_and_slope(x):
    kind = x.dtype
    c = lambda value: jnp.asarray(value, kind)
    square = x * x
    held = jnp.minimum(square, c(40.0))
    inner = x * (c(ERF[0]) + held * (c(ERF[1]) + held * c(ERF[2])))
    share = c(0.5) + c(0.5) * jnp.tanh(inner)
    bell = jnp.exp2(square * c(-0.5 * LOG2E))
    return x * share, share + x * (bell * c(PDF))


def fold(values):
    rows, width = values.shape
    return jnp.sum(values.reshape(rows // 8, 8, width), 0)


def spread(column, width):
    return jnp.concatenate([column] * (width // column.shape[1]), 1)


def normalize(values):
    centre = values - jnp.mean(values, -1, keepdims=True)
    scale = lax.rsqrt(jnp.mean(centre * centre, -1, keepdims=True) + 1e-05)
    return centre * scale, scale


def normalize_back(grad, normal, scale, gain):
    scaled = grad * gain
    return scale * (
        scaled
        - jnp.mean(scaled, -1, keepdims=True)
        - normal * jnp.mean(scaled * normal, -1, keepdims=True)
    )


WEIGHTS = ("wqkv", "wo", "ad", "au", "adb", "aub", "gain", "shift", "w1", "w2")
HELD = ("cst",) + WEIGHTS
STATE = (
    "qkv", "prob", "merged", "inv", "src0", "src1", "norm0", "norm1", "rs0", "rs1",
    "slope", "mid0", "mid1", "xin", "ready", "accm", "accv",
)
BIG = ("outs", "grads")
V_GAIN1, V_SHIFT1, V_UP1, V_GAIN0, V_SHIFT0, V_UP0, V_X, V_B1, V_B2, V_DOWN = range(10)
GROUP = 4
PART_ROWS = 72


def weave(main, *sides):
    rest = chain(*sides)
    for _ in main:
        next(rest, None)
    for _ in rest:
        pass


def step_kernel(names, sizes, spec, *refs):
    r = SimpleNamespace(**dict(zip(names, refs)))
    section = lax.axis_index("section")
    width, hidden, low = sizes
    pairs = width // PAIR
    seg = r.seg
    batches, slots = seg.shape
    per = slots // UNIT
    first = spec.first
    is_long = [seg[b, ITEM] == 0 for b in range(batches)]
    counts = [
        sum((seg[b, ITEM * k] >= 0).astype(jnp.int32) for k in range(slots // ITEM)) * ITEM
        for b in range(batches)
    ]

    def by_batch(values, batch):
        chosen = values[0]
        for b in range(1, batches):
            chosen = jnp.where(batch == b, values[b], chosen)
        return chosen

    def rows_of(u, count=UNIT):
        return pl.ds(pl.multiple_of(u * count, count), count)

    def share(which):
        first_, second = [jnp.int32(0 if v is None else v) for v in which]
        return jnp.where(section == 0, first_, second)

    def only(which, work):
        if which[0] is None or which[1] is None:
            pl.when(section == (0 if which[1] is None else 1))(work)
        else:
            work()

    def batch_copy(src, dst, at, sem):
        return pltpu.make_async_copy(src, dst.at[rows_of(at, slots)], sem)

    copies = []
    if spec.before:
        copies.append((spec.before, batch_copy(r.ready, r.grads, share(spec.before), r.sems.at[0])))
    if spec.done:
        rows = rows_of(share(spec.done), slots)
        copies.append((spec.done, pltpu.make_async_copy(r.xin.at[rows], r.outs.at[rows], r.sems.at[1])))
    for which, copy in copies:
        only(which, copy.start)
    takes = spec.a is not None and spec.a[1] is not None
    if takes:
        cot = pltpu.make_async_copy(r.cot.at[rows_of(spec.a[1], slots)], r.gin, r.sems.at[2])
        only((None, 0), cot.start)
    waits = {}
    if first:
        for i, name in enumerate(WEIGHTS):
            waits[name] = pltpu.make_async_copy(getattr(r, name + "_hbm"), getattr(r, name), r.sems.at[4 + i])
        parts = [
            pltpu.make_async_copy(r.tok.at[rows_of(b, slots)], r.xin.at[rows_of(b, slots)], r.sems.at[14 + b])
            for b in range(batches)
        ]
        parts[0].start()
        waits["wqkv"].start()
        r.accm[...] = jnp.zeros_like(r.accm)
        r.accv[...] = jnp.zeros_like(r.accv)
        row = lax.broadcasted_iota(jnp.int32, (2 * TILE, PAIR), 0)
        lane = lax.broadcasted_iota(jnp.int32, (2 * TILE, PAIR), 1)
        own = ((row // TILE) == (lane // (PAIR // 2))).astype(f32)
        item = (row % TILE) // ITEM
        cst = r.cst
        cst[0 : 2 * TILE, :] = own.astype(bf16)
        cst[2 * TILE : 4 * TILE, :] = (-own).astype(bf16)
        other = jnp.where((lane < TILE // ITEM) & (lane != item), 1.0, 0.0)
        cst[4 * TILE : 6 * TILE, :] = other.astype(bf16)
        cst[6 * TILE : 8 * TILE, :] = jnp.where(lane == item, -1e30, 0.0).astype(bf16)

    def arrive(*some):
        if first:
            for name in some:
                waits[name].wait()

    cst = r.cst

    def head_mask():
        return cst[0 : 2 * TILE, :]

    def block_k(rows, p):
        k = r.qkv[rows, pl.ds(pl.multiple_of(width + p * PAIR, PAIR), PAIR)]
        return jnp.concatenate([k, k], 0) * head_mask()

    def block_v(rows, p, back):
        v = r.qkv[rows, pl.ds(pl.multiple_of(2 * width + p * PAIR, PAIR), PAIR)]
        tail = cst[2 * TILE : 4 * TILE, :] if back else head_mask()
        return jnp.concatenate([jnp.concatenate([v, v], 0) * head_mask(), tail], 1)

    def lanes(p):
        return pl.ds(pl.multiple_of(p * PAIR, PAIR), PAIR)

    def softened(parts):
        tops = [
            jnp.max(jnp.concatenate([s[:, h * TILE : (h + 1) * TILE] for s in parts], 1), 1, keepdims=True)
            for h in range(2)
        ]
        return [
            jnp.concatenate(
                [jnp.exp2(s[:, h * TILE : (h + 1) * TILE] - tops[h]).astype(bf16) for h in range(2)], 1
            )
            for s in parts
        ]

    def finish_pair(rows, p, summed):
        inverse = 1.0 / summed[:, PAIR:]
        r.merged[rows, lanes(p)] = (summed[:, :PAIR] * inverse).astype(bf16)
        r.inv[rows, lanes(p)] = inverse.astype(bf16)

    def short_prob(u, t, p):
        return rows_of((u * (UNIT // TILE) + t) * pairs + p, TILE)

    def attend_short(u):
        def work(which):
            places = [(rows_of(u * (UNIT // TILE) + t, TILE), p, short_prob(u, t, p)) for p, t in which]
            scores = []
            for rows, p, _ in places:
                left = jnp.concatenate([r.qkv[rows, lanes(p)], cst[6 * TILE : 7 * TILE, :]], 1)
                right = jnp.concatenate([block_k(rows, p), cst[4 * TILE : 6 * TILE, :]], 1)
                scores.append(mm_t(left, right))
            probs = [softened([score])[0] for score in scores]
            values = [block_v(rows, p, False) for rows, p, _ in places]
            sums = [mm(prob, value) for prob, value in zip(probs, values)]
            for (rows, p, at), prob, summed in zip(places, probs, sums):
                r.prob[at, :] = prob
                finish_pair(rows, p, summed)

        work([(p, t) for p in range(pairs) for t in range(UNIT // TILE)])

    def long_tiles(u):
        base = (u // per) * per * (UNIT // TILE)
        return [rows_of(base + j, TILE) for j in range(3)]

    def attend_long(u):
        tiles = long_tiles(u)
        last = rows_of((u // per) * per * (UNIT // TILE) + 3, TILE)

        def some_pairs(i, _):
            which = [i * LONG_TOGETHER + q for q in range(LONG_TOGETHER)]
            keys = [[block_k(tile, p) for tile in tiles] for p in which]
            scores = [[[mm_t(r.qkv[rows, lanes(p)], key) for key in keys[n]] for rows in tiles] for n, p in enumerate(which)]
            values = [jnp.concatenate([block_v(tile, p, False) for tile in tiles], 0) for p in which]
            probs = [[softened(score) for score in some] for some in scores]
            sums = [[mm(jnp.concatenate(prob, 1), value) for prob in some] for some, value in zip(probs, values)]
            for n, p in enumerate(which):
                for rows, summed in zip(tiles, sums[n]):
                    finish_pair(rows, p, summed)
            return 0

        lax.fori_loop(0, pairs // LONG_TOGETHER, some_pairs, 0)
        r.merged[last, :] = jnp.zeros((TILE, width), bf16)
        r.inv[last, :] = jnp.zeros((TILE, width), bf16)

    def diagonal(values):
        half = PAIR // 2
        return jnp.concatenate([values[:half, :TILE], values[half:, TILE:]], 0).astype(bf16).T

    def scaled_out(rows, p):
        grad = r.src0[rows, lanes(p)] * r.inv[rows, lanes(p)]
        return grad, jnp.concatenate([grad, grad * r.merged[rows, lanes(p)]], 1)

    def put_fused(rows, p, dq, dk, dv):
        r.qkv[rows, lanes(p)] = (dq * (width // HEADS) ** -0.5).astype(bf16)
        r.qkv[rows, pl.ds(pl.multiple_of(width + p * PAIR, PAIR), PAIR)] = diagonal(dk * LN2)
        r.qkv[rows, pl.ds(pl.multiple_of(2 * width + p * PAIR, PAIR), PAIR)] = diagonal(dv)

    def attend_short_back(u):
        def work(which):
            places = [
                (rows_of(u * (UNIT // TILE) + t, TILE), p, short_prob(u, t, p))
                for p, t in which
            ]
            grads = [scaled_out(rows, p) for rows, p, _ in places]
            probs = [r.prob[at, :] for _, _, at in places]
            dscores = [mm_t(both, block_v(rows, p, True)) for (rows, p, _), (_, both) in zip(places, grads)]
            dvs = [mm(grad.T, prob) for (grad, _), prob in zip(grads, probs)]
            dscores = [score.astype(bf16) * prob for score, prob in zip(dscores, probs)]
            dqs = [mm(score, block_k(rows, p)) for (rows, p, _), score in zip(places, dscores)]
            dks = [mm(r.qkv[rows, lanes(p)].T, score) for (rows, p, _), score in zip(places, dscores)]
            for (rows, p, _), dq, dk, dv in zip(places, dqs, dks, dvs):
                put_fused(rows, p, dq, dk, dv)

        work([(p, t) for p in range(pairs) for t in range(UNIT // TILE)])

    def attend_long_back(u, lo, hi):
        tiles = long_tiles(u)

        def some_pairs(i, _):
            which = [i * LONG_TOGETHER + q for q in range(LONG_TOGETHER)]
            keys = [[block_k(tile, p) for tile in tiles] for p in which]
            values = [[block_v(tile, p, True) for tile in tiles] for p in which]
            scores = [[[mm_t(r.qkv[rows, lanes(p)], key) for key in keys[n]] for rows in tiles] for n, p in enumerate(which)]
            grads = [[scaled_out(rows, p) for rows in tiles] for p in which]
            slopes = [[[mm_t(both, value) for value in values[n]] for _, both in grads[n]] for n in range(LONG_TOGETHER)]
            turned = [jnp.concatenate([grad.T for grad, _ in some], 1) for some in grads]
            queries = [jnp.concatenate([r.qkv[rows, lanes(p)].T for rows in tiles], 1) for p in which]
            probs = [[softened(score) for score in some] for some in scores]
            dscores = [
                [[d.astype(bf16) * prob for d, prob in zip(*row)] for row in zip(*both)] for both in zip(slopes, probs)
            ]
            column = lambda table, j: jnp.concatenate([row[j] for row in table], 0)
            dvs = [[mm(turned[n], column(probs[n], j)) for j in range(3)] for n in range(LONG_TOGETHER)]
            dqs = [[mm(jnp.concatenate(row, 1), jnp.concatenate(keys[n], 0)) for row in dscores[n]] for n in range(LONG_TOGETHER)]
            dks = [[mm(queries[n], column(dscores[n], j)) for j in range(3)] for n in range(LONG_TOGETHER)]
            for n, p in enumerate(which):
                for j, rows in enumerate(tiles):
                    put_fused(rows, p, dqs[n][j], dks[n][j], dvs[n][j])
            return 0

        lax.fori_loop(lo, hi, some_pairs, 0)

    held = {}
    blocks = UNIT // BLOCK

    def local(h, b=None):
        return slice(h * UNIT, (h + 1) * UNIT) if b is None else slice(h * UNIT + b * BLOCK, h * UNIT + (b + 1) * BLOCK)

    def valid_of(batch, h, b):
        place = lax.broadcasted_iota(jnp.int32, (BLOCK, 1), 0) + (h * UNIT + b * BLOCK)
        return (place < by_batch(counts, batch)).astype(f32)

    def accumulate(index, values):
        r.accv[8 * index : 8 * index + 8, : values.shape[1]] += values

    def project(batch, h):
        rows = rows_of(batch * per + h)
        x = r.xin[rows, :]
        scale = (width // HEADS) ** -0.5 * LOG2E
        for j in range(0, 3 * width, 256):
            y = mm(x, r.wqkv[:, j : j + 256])
            if j < width:
                y = y * scale
            r.qkv[rows, j : j + 256] = y.astype(bf16)

    def adapter(which, values, rows):
        source = values.astype(bf16)
        (r.src0, r.src1)[which][rows, :] = source
        before = mm_t(source, r.ad[which]) + r.adb[which : which + 1, :]
        yield
        middle, slope = gelu_and_slope(before)
        middle = middle.astype(bf16)
        (r.mid0, r.mid1)[which][rows, :] = jnp.concatenate([middle, slope.astype(bf16)], 1)
        yield
        held["up"] = mm(middle, r.au[which])
        yield

    def before_ff(batch, h):
        u = batch * per + h
        rows = rows_of(u)
        attended = mm(r.merged[rows, :], r.wo[...])
        yield
        yield from adapter(0, attended, rows)
        up = held["up"]
        sums = [0.0, 0.0]
        for b in range(blocks):
            at = rows_of(u * blocks + b, BLOCK)
            here = slice(b * BLOCK, (b + 1) * BLOCK)
            branch = attended[here] + (up[here] + r.aub[0:1, :])
            x = r.xin[at, :].astype(f32)
            valid = valid_of(batch, h, b)
            sums[0] = sums[0] + fold(x * x * valid)
            sums[1] = sums[1] + fold(branch * branch * valid)
            normal, scale = normalize(x + branch)
            r.norm0[at, :] = normal.astype(bf16)
            r.rs0[at, :] = jnp.broadcast_to(scale, (BLOCK, 128))
            normed = normal * r.gain[0:1, :] + r.shift[0:1, :]
            r.keep[local(h, b), :] = normed
            r.low[local(h, b), :] = normed.astype(bf16)
            yield
        accumulate(V_X, sums[0])
        accumulate(V_B1, sums[1])

    def ff(batch, h):
        rows = rows_of(batch * per + h)
        normed = r.low[local(h), :]
        ahead = mm(normed, r.w1[:, :256])
        act = total = None
        for j in range(0, hidden, 256):
            now = ahead
            if j + 256 < hidden:
                ahead = mm(normed, r.w1[:, j + 256 : j + 512])
            if j == 256 and h == 0:
                arrive("w2")
            if j:
                part = mm(act, r.w2[j - 256 : j, :])
                total = part if j == 256 else total + part
            act, slope = gelu_and_slope(now.astype(bf16))
            r.slope[rows, j : j + 256] = slope
            yield
        held[h] = total + mm(act, r.w2[hidden - 256 :, :])

    def after_ff(batch, h):
        u = batch * per + h
        rows = rows_of(u)
        expanded = held[h]
        yield from adapter(1, expanded, rows)
        up = held["up"]
        square = 0.0
        for b in range(blocks):
            at = rows_of(u * blocks + b, BLOCK)
            here = slice(b * BLOCK, (b + 1) * BLOCK)
            branch = expanded[here] + (up[here] + r.aub[1:2, :])
            valid = valid_of(batch, h, b)
            square = square + fold(branch * branch * valid)
            normal, scale = normalize(r.keep[local(h, b), :] + branch)
            r.norm1[at, :] = normal.astype(bf16)
            r.rs1[at, :] = jnp.broadcast_to(scale, (BLOCK, 128))
            result = ((normal * r.gain[1:2, :] + r.shift[1:2, :]) * valid).astype(bf16)
            r.xin[at, :] = result
            if hasattr(r, "send"):
                r.send[local(h, b), :] = result
            yield
        accumulate(V_B2, square)

    def adapter_back(which, rows, h):
        up = r.low[local(h), :]
        both = (r.mid0, r.mid1)[which][rows, :]
        middle, slope = both[:, :low], both[:, low:]
        before = (mm_t(up, r.au[which]) * slope.astype(f32)).astype(bf16)
        yield
        into = mm(before, r.ad[which])
        yield
        source = (r.src0, r.src1)[which][rows, :]
        flat = jnp.concatenate([middle, before], 1).T
        r.accm[(2 + which) * low : (3 + which) * low, :] += mm(flat[:low, :], up)
        r.accm[which * low : (which + 1) * low, :] += mm(flat[low:, :], source)
        yield
        accumulate(V_UP1 if which else V_UP0, fold(up.astype(f32)))
        side = jnp.zeros((UNIT, low), f32)
        wide = [side, before.astype(f32)] if which else [before.astype(f32), side]
        accumulate(V_DOWN, fold(jnp.concatenate(wide, 1)))
        held["into"] = (r.keep[local(h), :] + into).astype(bf16)
        yield

    def before_ff_back(batch, h):
        u = batch * per + h
        sums = [0.0, 0.0]
        for b in range(blocks):
            at = rows_of(u * blocks + b, BLOCK)
            grad = r.gin[local(h, b), :].astype(f32) * valid_of(batch, h, b)
            normal = r.norm1[at, :].astype(f32)
            sums[0] = sums[0] + fold(grad * normal)
            sums[1] = sums[1] + fold(grad)
            grad = normalize_back(grad, normal, spread(r.rs1[at, :], width), r.gain[1:2, :])
            r.keep[local(h, b), :] = grad
            r.low[local(h, b), :] = grad.astype(bf16)
            yield
        accumulate(V_GAIN1, sums[0])
        accumulate(V_SHIFT1, sums[1])
        yield from adapter_back(1, rows_of(u), h)
        held[h] = held["into"]

    def ff_back(batch, h):
        rows = rows_of(batch * per + h)
        down = held[h]
        ahead = mm_t(down, r.w2[:256, :])
        dhidden = total = None
        for j in range(0, hidden, 256):
            now = ahead
            if j + 256 < hidden:
                ahead = mm_t(down, r.w2[j + 256 : j + 512, :])
            if j:
                part = mm_t(dhidden, r.w1[:, j - 256 : j])
                total = part if j == 256 else total + part
            dhidden = now.astype(bf16) * r.slope[rows, j : j + 256]
            yield
        held[h] = r.keep[local(h), :] + (total + mm_t(dhidden, r.w1[:, hidden - 256 :]))

    def after_ff_back(batch, h):
        u = batch * per + h
        total = held[h]
        sums = [0.0, 0.0]
        for b in range(blocks):
            at = rows_of(u * blocks + b, BLOCK)
            grad = total[b * BLOCK : (b + 1) * BLOCK]
            normal = r.norm0[at, :].astype(f32)
            sums[0] = sums[0] + fold(grad * normal)
            sums[1] = sums[1] + fold(grad)
            grad = normalize_back(grad, normal, spread(r.rs0[at, :], width), r.gain[0:1, :])
            upper = grad.astype(bf16)
            r.norm0[at, :] = upper
            r.norm1[at, :] = (grad - upper.astype(f32)).astype(bf16)
            r.keep[local(h, b), :] = grad
            r.low[local(h, b), :] = upper
            yield
        accumulate(V_GAIN0, sums[0])
        accumulate(V_SHIFT0, sums[1])
        yield from adapter_back(0, rows_of(u), h)
        r.src0[rows_of(u), :] = held["into"]

    def to_merged(batch, h):
        rows = rows_of(batch * per + h)
        grad = r.src0[rows, :]
        parts_ = []
        for j in range(0, width, 256):
            parts_.append(mm_t(grad, r.wo[j : j + 256, :]).astype(bf16))
            yield
        r.src0[rows, :] = jnp.concatenate(parts_, 1)

    def to_input(batch, h):
        rows = rows_of(batch * per + h)
        for j in range(0, width, 256):
            part = mm_t(r.qkv[rows, :], r.wqkv[j : j + 256, :])
            part = part + r.norm0[rows, j : j + 256].astype(f32)
            r.ready[local(h), j : j + 256] = part + r.norm1[rows, j : j + 256].astype(f32)

    def forward_front(batch):
        for h in range(per):
            project(batch, h)
        long = by_batch(is_long, batch)

        @pl.when(jnp.logical_not(long))
        def _():
            for h in range(per):
                attend_short(batch * per + h)

        @pl.when(long)
        def _():
            attend_long(batch * per)

    def forward_rest(batch):
        arrive(*WEIGHTS[1:8])
        weave(before_ff(batch, 0))
        arrive("w1")
        weave(ff(batch, 0), before_ff(batch, 1))
        weave(ff(batch, 1), after_ff(batch, 0))
        weave(after_ff(batch, 1))

    def backward_rest(batch, merges):
        weave(before_ff_back(batch, 0))
        weave(ff_back(batch, 0), before_ff_back(batch, 1))
        weave(ff_back(batch, 1), after_ff_back(batch, 0))
        if merges:
            weave(after_ff_back(batch, 1), to_merged(batch, 0))
            weave(to_merged(batch, 1))
        else:
            weave(after_ff_back(batch, 1))

    def attention_back(batch, part):
        long = by_batch(is_long, batch)
        some = range(per) if part is None else (part,)

        def out(h):
            return pltpu.make_async_copy(r.ready.at[local(h)], r.grads.at[rows_of(batch * per + h)], r.sems.at[h])

        @pl.when(jnp.logical_not(long))
        def _():
            if part is not None:
                weave(to_merged(batch, part))
            for h in some:
                attend_short_back(batch * per + h)
            if part is not None:
                to_input(batch, part)
                out(part).start()
                out(part).wait()

        @pl.when(long)
        def _():
            if part == 0:
                for h in range(per):
                    weave(to_merged(batch, h))
            end = pairs // LONG_TOGETHER
            attend_long_back(batch * per, EARLY if part == 1 else 0, EARLY if part == 0 else end)
            if part != 0:
                r.qkv[rows_of(batch * per * (UNIT // TILE) + 3, TILE), :] = jnp.zeros((TILE, 3 * width), bf16)
            if part == 1:
                for h in range(per):
                    to_input(batch, h)
                    out(h).start()
                for h in range(per):
                    out(h).wait()

    if first:
        parts[0].wait()
        waits["wqkv"].wait()
        for name in WEIGHTS[1:]:
            waits[name].start()
        for copy in parts[1:]:
            copy.start()

        @pl.when(section == 0)
        def _():
            forward_front(0)
            forward_rest(0)

        @pl.when(section != 0)
        def _():
            arrive(*WEIGHTS[1:])

        for copy in parts[1:]:
            copy.wait()
    elif spec.f is not None:

        def whole_forward():
            batch = share(spec.f)

            @pl.when(section != 0)
            def _():
                r.xin[rows_of(batch, slots), :] = r.recv[...]

            forward_front(batch)
            forward_rest(batch)

        only(spec.f, whole_forward)
    if spec.a is not None:
        if takes:
            only((None, 0), cot.wait)
        if spec.a[0] is not None:
            @pl.when(section == 0)
            def _():
                r.gin[...] = r.recv[...]

        only(spec.a, lambda: backward_rest(share(spec.a), spec.b is not None))

    for which, copy in copies:
        only(which, copy.wait)
    if spec.part is not None:
        only(spec.b, lambda: attention_back(share(spec.b), spec.part))
    elif spec.b is not None:
        batch_b = share(spec.b)

        def whole_back():
            attention_back(batch_b, None)
            for h in range(per):
                to_input(batch_b, h)

            r.send[...] = r.ready[...].astype(bf16)

        only(spec.b, whole_back)
    if spec.pay:
        whole = r.whole
        whole[0 : 4 * low, :] = r.accm[...]
        vectors = [jnp.sum(r.accv[8 * i : 8 * i + 8, :], 0, keepdims=True) for i in range(10)]
        total = counts[0]
        for b in range(1, batches):
            total = total + counts[b]
        vectors.append(jnp.full((1, width), total.astype(f32)))
        vectors.append(jnp.zeros((GROUP * PART_ROWS - 4 * low - len(vectors), width), f32))
        whole[4 * low :, :] = jnp.concatenate(vectors, 0)
        place = lax.axis_index("dp") % GROUP
        for o in range(GROUP):
            part = whole[rows_of(jnp.bitwise_xor(place, o), PART_ROWS), :]
            (r.part0, r.part1, r.part2, r.part3)[o][...] = part if o == 0 else part.astype(bf16)


def add_kernel(count, *refs):
    total = refs[0][...]
    for ref in refs[1 : 1 + count]:
        total = total + ref[...].astype(f32)
    refs[-2][...] = total
    refs[-1][...] = total.astype(bf16)


def finish_kernel(low, *refs):
    parts, (down, down_bias, up, up_bias, gain, shift, stats, whole) = refs[:GROUP], refs[GROUP:]
    place = lax.axis_index("dp") % GROUP
    for o in range(GROUP):
        at = pl.multiple_of(jnp.bitwise_xor(place, o) * PART_ROWS, PART_ROWS)
        whole[pl.ds(at, PART_ROWS), :] = parts[o][...].astype(f32)
    width = whole.shape[1]
    for k in range(2):
        down[k] = whole[k * low : (k + 1) * low, :]
        up[k] = whole[(2 + k) * low : (3 + k) * low, :]
    base = 4 * low
    row = lambda i: whole[base + i : base + i + 1, :]
    for out, pair in ((up_bias, (V_UP0, V_UP1)), (gain, (V_GAIN0, V_GAIN1)), (shift, (V_SHIFT0, V_SHIFT1))):
        for k in range(2):
            out[k : k + 1, :] = row(pair[k])
    for k in range(2):
        down_bias[k : k + 1, :] = row(V_DOWN)[:, k * low : (k + 1) * low]
    sums = [jnp.sum(row(i), 1, keepdims=True) for i in (V_X, V_B1, V_B2)]
    stats[...] = jnp.sqrt(jnp.concatenate(sums, 1) / (row(10)[:, :1] * width))


VSPEC = pl.BlockSpec(memory_space=pltpu.VMEM)
ASPEC = pl.BlockSpec(memory_space=pl.ANY)
SSPEC = pl.BlockSpec(memory_space=pltpu.SMEM)


def hbm(value):
    return pltpu.with_memory_space_constraint(value, pltpu.HBM)


def vmem(value):
    return pltpu.with_memory_space_constraint(value, pltpu.VMEM)


def run_step(
    env, name, first=False, f=None, a=None, b=None, part=None, before=None, done=None, send=True, pay=False, through=None
):
    spec = SimpleNamespace(first=first, f=f, a=a, b=b, part=part, before=before, done=done, pay=pay)
    shapes = env.shapes
    width, hidden = shapes["w1"][0]
    sizes = (width, hidden, shapes["adb"][0][1])
    ins, in_names, in_specs = [hbm(env.seg)], ["seg"], [SSPEC]
    if first:
        for n in HELD:
            if n != "cst":
                ins.append(hbm(getattr(env, n)))
                in_names.append(n + "_hbm")
                in_specs.append(ASPEC)
    else:
        for n in HELD:
            ins.append(vmem(getattr(env, n)))
            in_names.append(n)
            in_specs.append(VSPEC)
        if a is not None and a[1] is not None:
            ins.append(hbm(env.cot))
            in_names.append("cot")
            in_specs.append(ASPEC)
        if f is not None or a is not None:
            ins.append(vmem(env.recv))
            in_names.append("recv")
            in_specs.append(VSPEC)
    if first:
        ins.append(hbm(env.tok))
        in_names.append("tok")
        in_specs.append(ASPEC)
    outs, out_names, out_specs, alias = [], [], [], {}
    if first:
        for n in HELD:
            outs.append(pltpu.VMEM(*shapes[n]))
            out_names.append(n)
            out_specs.append(VSPEC)
    for n in STATE:
        if not first:
            alias[len(ins)] = len(outs)
            ins.append(vmem(getattr(env, n)))
            in_names.append("old_" + n)
            in_specs.append(VSPEC)
        outs.append(pltpu.VMEM(*shapes[n]))
        out_names.append(n)
        out_specs.append(VSPEC)
    for n in BIG:
        if (n == "outs" and done is None) or (n == "grads" and before is None and part is None):
            continue
        if hasattr(env, n):
            alias[len(ins)] = len(outs)
            ins.append(getattr(env, n))
            in_names.append("old_" + n)
            in_specs.append(ASPEC)
        outs.append(pltpu.HBM(*shapes[n]))
        out_names.append(n)
        out_specs.append(ASPEC)
    if through is not None:
        alias[len(ins)] = len(outs)
        ins.append(vmem(through))
        in_names.append("old_through")
        in_specs.append(VSPEC)
        outs.append(pltpu.VMEM(through.shape, through.dtype))
        out_names.append("through")
        out_specs.append(VSPEC)
    if send:
        outs.append(jax.ShapeDtypeStruct((2 * UNIT, width), bf16))
        out_names.append("send")
        out_specs.append(VSPEC)
    if pay:
        for o in range(GROUP):
            outs.append(jax.ShapeDtypeStruct((PART_ROWS, width), bf16 if o else f32))
            out_names.append("part%d" % o)
            out_specs.append(VSPEC)
    scratch = {
        "keep": pltpu.VMEM((2 * UNIT, width), f32),
        "low": pltpu.VMEM((2 * UNIT, width), bf16),
        "gin": pltpu.VMEM((2 * UNIT, width), bf16),
        "sems": pltpu.SemaphoreType.DMA((16,)),
    }
    if pay:
        scratch["whole"] = pltpu.VMEM((GROUP * PART_ROWS, width), f32)
    names = in_names + out_names + list(scratch)
    flops = 2 * 2 * UNIT * width * (9 * width + 2 * hidden)
    results = pl.pallas_call(
        partial(step_kernel, names, sizes, spec),
        out_shape=tuple(outs),
        in_specs=in_specs,
        out_specs=tuple(out_specs),
        scratch_shapes=list(scratch.values()),
        input_output_aliases=alias,
        compiler_params=pltpu.CompilerParams(vmem_limit_bytes=SCOPED),
        cost_estimate=pl.CostEstimate(flops=flops, bytes_accessed=2**20, transcendentals=0),
        name=name,
    )(*ins)
    vars(env).update(zip(out_names, results))


def swapped(value, axis, mask):
    count = lax.axis_size(axis)
    return lax.ppermute(value, axis, [(i, i ^ mask) for i in range(count)])


def add_up(total, terms, name):
    shape = total.shape
    return pl.pallas_call(
        partial(add_kernel, len(terms)),
        out_shape=(jax.ShapeDtypeStruct(shape, f32), jax.ShapeDtypeStruct(shape, bf16)),
        in_specs=[VSPEC] * (1 + len(terms)),
        out_specs=(VSPEC, VSPEC),
        compiler_params=pltpu.CompilerParams(vmem_limit_bytes=SCOPED),
        name=name,
    )(total, *terms)


def make_shapes(env):
    rows, width = env.tok.shape
    hidden = env.w1.shape[1]
    low = env.au.shape[1]
    shapes = {n: (getattr(env, n).shape, getattr(env, n).dtype) for n in HELD if n != "cst"}
    shapes["cst"] = ((8 * TILE, PAIR), bf16)
    wide = ((rows, width), bf16)
    for n in ("merged", "inv", "src0", "src1", "norm0", "norm1", "xin", "outs"):
        shapes[n] = wide
    shapes["qkv"] = ((rows, 3 * width), bf16)
    shapes["prob"] = ((rows * (width // PAIR), 2 * TILE), bf16)
    shapes["rs0"] = shapes["rs1"] = ((rows, 128), f32)
    shapes["slope"] = ((rows, hidden), bf16)
    shapes["mid0"] = shapes["mid1"] = ((rows, 2 * low), bf16)
    shapes["ready"] = ((2 * UNIT, width), f32)
    shapes["grads"] = ((rows, width), f32)
    shapes["accm"] = ((4 * low, width), f32)
    shapes["accv"] = ((80, width), f32)
    return shapes


def local(
    tokens,
    segment_ids,
    w_qkv,
    w_attn_out,
    w_ff_in,
    w_ff_out,
    adapter_down,
    adapter_down_bias,
    adapter_up,
    adapter_up_bias,
    ln_gain,
    ln_bias,
    cotangent,
):
    batches, slots, width = tokens.shape
    low = adapter_down.shape[3]
    rows = batches * slots
    env = SimpleNamespace(
        seg=segment_ids,
        tok=tokens.reshape(rows, width),
        cot=cotangent.reshape(rows, width),
        wqkv=w_qkv[0],
        wo=w_attn_out[0],
        w1=w_ff_in[0],
        w2=w_ff_out[0],
        ad=jnp.swapaxes(adapter_down[0], 1, 2),
        au=adapter_up[0],
        adb=adapter_down_bias[0],
        aub=adapter_up_bias[0],
        gain=ln_gain[0],
        shift=ln_bias[0],
    )
    env.shapes = make_shapes(env)

    def swap():
        return lax.ppermute(env.send, "section", [(0, 1), (1, 0)])

    run_step(env, "relay0", first=True, f=(0, None))
    env.recv = swap()
    run_step(env, "relay1", f=(1, 0), done=(0, None))
    inputs = swap()
    run_step(env, "relay2", a=(None, 0), b=(None, 0), done=(1, 0))
    gradient = swap()
    env.recv = inputs
    run_step(env, "relay3", f=(None, 1), before=(None, 0), send=False)
    env.recv = gradient
    run_step(env, "relay4", a=(0, 1), b=(0, 1), done=(None, 1))
    env.recv = swap()
    run_step(env, "relay5", a=(1, None), before=(0, 1), send=False, pay=True)
    got = [swapped(part, "dp", o + 1) for o, part in enumerate((env.part1, env.part2, env.part3))]
    total, short = add_up(env.part0, got, "add0")
    mask = GROUP
    count = lax.axis_size("dp")
    while mask < count:
        got = swapped(short, "dp", mask)
        if 2 * mask >= count:
            run_step(env, "tail0", b=(1, None), part=0, send=False, through=total)
            total = env.through
        total, short = add_up(total, [got], "add%d" % mask)
        mask *= 2
    got = [swapped(short, "dp", o) for o in range(1, GROUP)]
    run_step(env, "tail1", b=(1, None), part=1, send=False)
    two = jax.ShapeDtypeStruct((2, width), f32)
    matrix = jax.ShapeDtypeStruct((2, low, width), f32)
    down, down_bias, up, up_bias, gain, shift, rms_stats = pl.pallas_call(
        partial(finish_kernel, low),
        out_shape=(matrix, jax.ShapeDtypeStruct((2, low), f32), matrix, two, two, two, jax.ShapeDtypeStruct((1, 3), f32)),
        in_specs=[VSPEC] * GROUP,
        out_specs=(VSPEC,) * 7,
        scratch_shapes=[pltpu.VMEM((GROUP * PART_ROWS, width), f32)],
        compiler_params=pltpu.CompilerParams(vmem_limit_bytes=SCOPED),
        name="finish",
    )(short, *got)
    return (
        env.outs.reshape(1, batches, slots, width),
        env.grads.reshape(1, batches, slots, width),
        jnp.swapaxes(down, 1, 2)[None],
        down_bias[None],
        up[None],
        up_bias[None],
        gain[None],
        shift[None],
        rms_stats,
    )


def solution(mesh):
    placed = (
        P(None, "dp", None),
        P(None, "dp"),
        P("section", None, None),
        P("section", None, None),
        P("section", None, None),
        P("section", None, None),
        P("section", None, None, None),
        P("section", None, None),
        P("section", None, None, None),
        P("section", None, None),
        P("section", None, None),
        P("section", None, None),
        P(None, "dp", None),
    )
    return jax.shard_map(
        local,
        mesh=mesh,
        in_specs=placed,
        out_specs=(
            P("section", None, "dp", None),
            P("section", None, "dp", None),
            P("section", None, None, None),
            P("section", None, None),
            P("section", None, None, None),
            P("section", None, None),
            P("section", None, None),
            P("section", None, None),
            P("section", None),
        ),
        check_vma=False,
    )
```

```python
from functools import partial
from itertools import chain
from types import SimpleNamespace

import jax
import jax.numpy as jnp
from jax import lax
from jax.experimental import pallas as pl
from jax.experimental.pallas import tpu as pltpu
from jax.sharding import PartitionSpec as P

HEADS = 12
ITEM = 32
UNIT = 256
TILE = 128
PAIR = 128
LOG2E = 1.4426950408889634
SCOPED = 9 * 2**20
BLOCK = 128
LONG_TOGETHER = 2
EARLY = 2
LN2 = 0.6931471805599453
bf16 = jnp.bfloat16
f32 = jnp.float32

ERF = (0.7977178338317933, 0.03679825608874024, -0.00031580706578781924)
PDF = 0.3989422804014327


def mm(left, right):
    return lax.dot_general(left, right, (((1,), (0,)), ((), ())), preferred_element_type=f32)


def mm_t(left, right):
    return lax.dot_general(left, right, (((1,), (1,)), ((), ())), preferred_element_type=f32)


def gelu_and_slope(x):
    kind = x.dtype
    c = lambda value: jnp.asarray(value, kind)
    square = x * x
    held = jnp.minimum(square, c(40.0))
    inner = x * (c(ERF[0]) + held * (c(ERF[1]) + held * c(ERF[2])))
    share = c(0.5) + c(0.5) * jnp.tanh(inner)
    bell = jnp.exp2(square * c(-0.5 * LOG2E))
    return x * share, share + x * (bell * c(PDF))


def fold(values):
    rows, width = values.shape
    return jnp.sum(values.reshape(rows // 8, 8, width), 0)


def spread(column, width):
    return jnp.concatenate([column] * (width // column.shape[1]), 1)


def normalize(values):
    centre = values - jnp.mean(values, -1, keepdims=True)
    scale = lax.rsqrt(jnp.mean(centre * centre, -1, keepdims=True) + 1e-05)
    return centre * scale, scale


def normalize_back(grad, normal, scale, gain):
    scaled = grad * gain
    return scale * (
        scaled
        - jnp.mean(scaled, -1, keepdims=True)
        - normal * jnp.mean(scaled * normal, -1, keepdims=True)
    )


WEIGHTS = ("wqkv", "wo", "ad", "au", "adb", "aub", "gain", "shift", "w1", "w2")
HELD = ("cst",) + WEIGHTS
STATE = (
    "qkv", "prob", "merged", "inv", "src0", "src1", "norm0", "norm1", "rs0", "rs1",
    "slope", "mid0", "mid1", "xin", "gin", "ready", "accm", "accv",
)
BIG = ("outs", "grads")
V_GAIN1, V_SHIFT1, V_UP1, V_GAIN0, V_SHIFT0, V_UP0, V_X, V_B1, V_B2, V_DOWN = range(10)
GROUP = 4
PART_ROWS = 72


def weave(main, *sides):
    rest = chain(*sides)
    for _ in main:
        next(rest, None)
    for _ in rest:
        pass


def step_kernel(names, sizes, spec, *refs):
    r = SimpleNamespace(**dict(zip(names, refs)))
    section = lax.axis_index("section")
    width, hidden, low = sizes
    pairs = width // PAIR
    seg = r.seg
    batches, slots = seg.shape
    per = slots // UNIT
    first = spec.first
    is_long = [seg[b, ITEM] == 0 for b in range(batches)]
    counts = [
        sum((seg[b, ITEM * k] >= 0).astype(jnp.int32) for k in range(slots // ITEM)) * ITEM
        for b in range(batches)
    ]

    def by_batch(values, batch):
        chosen = values[0]
        for b in range(1, batches):
            chosen = jnp.where(batch == b, values[b], chosen)
        return chosen

    def rows_of(u, count=UNIT):
        return pl.ds(pl.multiple_of(u * count, count), count)

    def share(which):
        first_, second = [jnp.int32(0 if v is None else v) for v in which]
        return jnp.where(section == 0, first_, second)

    def only(which, work):
        if which[0] is None or which[1] is None:
            pl.when(section == (0 if which[1] is None else 1))(work)
        else:
            work()

    def batch_copy(src, dst, at, sem):
        return pltpu.make_async_copy(src, dst.at[rows_of(at, slots)], sem)

    copies = []
    if spec.before:
        copies.append((spec.before, batch_copy(r.ready, r.grads, share(spec.before), r.sems.at[0])))
    if spec.done:
        rows = rows_of(share(spec.done), slots)
        copies.append((spec.done, pltpu.make_async_copy(r.xin.at[rows], r.outs.at[rows], r.sems.at[1])))
    if spec.cot is not None:
        cot = pltpu.make_async_copy(r.cot.at[rows_of(spec.cot, slots)], r.gin, r.sems.at[2])
        copies.append(((None, 0), cot))
    for which, copy in copies:
        only(which, copy.start)
    waits = {}
    if first:
        for i, name in enumerate(WEIGHTS):
            waits[name] = pltpu.make_async_copy(getattr(r, name + "_hbm"), getattr(r, name), r.sems.at[4 + i])
        parts = [
            pltpu.make_async_copy(r.tok.at[rows_of(b, slots)], r.xin.at[rows_of(b, slots)], r.sems.at[14 + b])
            for b in range(batches)
        ]
        parts[0].start()
        waits["wqkv"].start()
        r.accm[...] = jnp.zeros_like(r.accm)
        r.accv[...] = jnp.zeros_like(r.accv)
        row = lax.broadcasted_iota(jnp.int32, (2 * TILE, PAIR), 0)
        lane = lax.broadcasted_iota(jnp.int32, (2 * TILE, PAIR), 1)
        own = ((row // TILE) == (lane // (PAIR // 2))).astype(f32)
        item = (row % TILE) // ITEM
        cst = r.cst
        cst[0 : 2 * TILE, :] = own.astype(bf16)
        cst[2 * TILE : 4 * TILE, :] = (-own).astype(bf16)
        other = jnp.where((lane < TILE // ITEM) & (lane != item), 1.0, 0.0)
        cst[4 * TILE : 6 * TILE, :] = other.astype(bf16)
        cst[6 * TILE : 8 * TILE, :] = jnp.where(lane == item, -1e30, 0.0).astype(bf16)

    def arrive(*some):
        if first:
            for name in some:
                waits[name].wait()

    cst = r.cst

    def head_mask():
        return cst[0 : 2 * TILE, :]

    def block_k(rows, p):
        k = r.qkv[rows, pl.ds(pl.multiple_of(width + p * PAIR, PAIR), PAIR)]
        return jnp.concatenate([k, k], 0) * head_mask()

    def block_v(rows, p, back):
        v = r.qkv[rows, pl.ds(pl.multiple_of(2 * width + p * PAIR, PAIR), PAIR)]
        tail = cst[2 * TILE : 4 * TILE, :] if back else head_mask()
        return jnp.concatenate([jnp.concatenate([v, v], 0) * head_mask(), tail], 1)

    def lanes(p):
        return pl.ds(pl.multiple_of(p * PAIR, PAIR), PAIR)

    def softened(parts):
        tops = [
            jnp.max(jnp.concatenate([s[:, h * TILE : (h + 1) * TILE] for s in parts], 1), 1, keepdims=True)
            for h in range(2)
        ]
        return [
            jnp.concatenate(
                [jnp.exp2(s[:, h * TILE : (h + 1) * TILE] - tops[h]).astype(bf16) for h in range(2)], 1
            )
            for s in parts
        ]

    def finish_pair(rows, p, summed):
        inverse = 1.0 / summed[:, PAIR:]
        r.merged[rows, lanes(p)] = (summed[:, :PAIR] * inverse).astype(bf16)
        r.inv[rows, lanes(p)] = inverse.astype(bf16)

    def short_prob(u, t, p):
        return rows_of((u * (UNIT // TILE) + t) * pairs + p, TILE)

    def attend_short(u):
        def work(which):
            places = [(rows_of(u * (UNIT // TILE) + t, TILE), p, short_prob(u, t, p)) for p, t in which]
            scores = []
            for rows, p, _ in places:
                left = jnp.concatenate([r.qkv[rows, lanes(p)], cst[6 * TILE : 7 * TILE, :]], 1)
                right = jnp.concatenate([block_k(rows, p), cst[4 * TILE : 6 * TILE, :]], 1)
                scores.append(mm_t(left, right))
            probs = [softened([score])[0] for score in scores]
            values = [block_v(rows, p, False) for rows, p, _ in places]
            sums = [mm(prob, value) for prob, value in zip(probs, values)]
            for (rows, p, at), prob, summed in zip(places, probs, sums):
                r.prob[at, :] = prob
                finish_pair(rows, p, summed)

        work([(p, t) for p in range(pairs) for t in range(UNIT // TILE)])

    def long_tiles(u):
        base = (u // per) * per * (UNIT // TILE)
        return [rows_of(base + j, TILE) for j in range(3)]

    def attend_long(u):
        tiles = long_tiles(u)
        last = rows_of((u // per) * per * (UNIT // TILE) + 3, TILE)

        def some_pairs(i, _):
            which = [i * LONG_TOGETHER + q for q in range(LONG_TOGETHER)]
            keys = [[block_k(tile, p) for tile in tiles] for p in which]
            scores = [[[mm_t(r.qkv[rows, lanes(p)], key) for key in keys[n]] for rows in tiles] for n, p in enumerate(which)]
            values = [jnp.concatenate([block_v(tile, p, False) for tile in tiles], 0) for p in which]
            probs = [[softened(score) for score in some] for some in scores]
            sums = [[mm(jnp.concatenate(prob, 1), value) for prob in some] for some, value in zip(probs, values)]
            for n, p in enumerate(which):
                for rows, summed in zip(tiles, sums[n]):
                    finish_pair(rows, p, summed)
            return 0

        lax.fori_loop(0, pairs // LONG_TOGETHER, some_pairs, 0)
        r.merged[last, :] = jnp.zeros((TILE, width), bf16)
        r.inv[last, :] = jnp.zeros((TILE, width), bf16)

    def diagonal(values):
        half = PAIR // 2
        return jnp.concatenate([values[:half, :TILE], values[half:, TILE:]], 0).astype(bf16).T

    def scaled_out(rows, p):
        grad = r.src0[rows, lanes(p)] * r.inv[rows, lanes(p)]
        return grad, jnp.concatenate([grad, grad * r.merged[rows, lanes(p)]], 1)

    def put_fused(rows, p, dq, dk, dv):
        r.qkv[rows, lanes(p)] = (dq * (width // HEADS) ** -0.5).astype(bf16)
        r.qkv[rows, pl.ds(pl.multiple_of(width + p * PAIR, PAIR), PAIR)] = diagonal(dk * LN2)
        r.qkv[rows, pl.ds(pl.multiple_of(2 * width + p * PAIR, PAIR), PAIR)] = diagonal(dv)

    def attend_short_back(u):
        def work(which):
            places = [
                (rows_of(u * (UNIT // TILE) + t, TILE), p, short_prob(u, t, p))
                for p, t in which
            ]
            grads = [scaled_out(rows, p) for rows, p, _ in places]
            probs = [r.prob[at, :] for _, _, at in places]
            dscores = [mm_t(both, block_v(rows, p, True)) for (rows, p, _), (_, both) in zip(places, grads)]
            dvs = [mm(grad.T, prob) for (grad, _), prob in zip(grads, probs)]
            dscores = [score.astype(bf16) * prob for score, prob in zip(dscores, probs)]
            dqs = [mm(score, block_k(rows, p)) for (rows, p, _), score in zip(places, dscores)]
            dks = [mm(r.qkv[rows, lanes(p)].T, score) for (rows, p, _), score in zip(places, dscores)]
            for (rows, p, _), dq, dk, dv in zip(places, dqs, dks, dvs):
                put_fused(rows, p, dq, dk, dv)

        work([(p, t) for p in range(pairs) for t in range(UNIT // TILE)])

    def attend_long_back(u, lo, hi):
        tiles = long_tiles(u)

        def some_pairs(i, _):
            which = [i * LONG_TOGETHER + q for q in range(LONG_TOGETHER)]
            keys = [[block_k(tile, p) for tile in tiles] for p in which]
            values = [[block_v(tile, p, True) for tile in tiles] for p in which]
            scores = [[[mm_t(r.qkv[rows, lanes(p)], key) for key in keys[n]] for rows in tiles] for n, p in enumerate(which)]
            grads = [[scaled_out(rows, p) for rows in tiles] for p in which]
            slopes = [[[mm_t(both, value) for value in values[n]] for _, both in grads[n]] for n in range(LONG_TOGETHER)]
            turned = [jnp.concatenate([grad.T for grad, _ in some], 1) for some in grads]
            queries = [jnp.concatenate([r.qkv[rows, lanes(p)].T for rows in tiles], 1) for p in which]
            probs = [[softened(score) for score in some] for some in scores]
            dscores = [
                [[d.astype(bf16) * prob for d, prob in zip(*row)] for row in zip(*both)] for both in zip(slopes, probs)
            ]
            column = lambda table, j: jnp.concatenate([row[j] for row in table], 0)
            dvs = [[mm(turned[n], column(probs[n], j)) for j in range(3)] for n in range(LONG_TOGETHER)]
            dqs = [[mm(jnp.concatenate(row, 1), jnp.concatenate(keys[n], 0)) for row in dscores[n]] for n in range(LONG_TOGETHER)]
            dks = [[mm(queries[n], column(dscores[n], j)) for j in range(3)] for n in range(LONG_TOGETHER)]
            for n, p in enumerate(which):
                for j, rows in enumerate(tiles):
                    put_fused(rows, p, dqs[n][j], dks[n][j], dvs[n][j])
            return 0

        lax.fori_loop(lo, hi, some_pairs, 0)

    held = {}
    blocks = UNIT // BLOCK

    def local(h, b=None):
        return slice(h * UNIT, (h + 1) * UNIT) if b is None else slice(h * UNIT + b * BLOCK, h * UNIT + (b + 1) * BLOCK)

    def valid_of(batch, h, b):
        place = lax.broadcasted_iota(jnp.int32, (BLOCK, 1), 0) + (h * UNIT + b * BLOCK)
        return (place < by_batch(counts, batch)).astype(f32)

    def accumulate(index, values):
        r.accv[8 * index : 8 * index + 8, : values.shape[1]] += values

    def project(batch, h):
        rows = rows_of(batch * per + h)
        x = r.xin[rows, :]
        scale = (width // HEADS) ** -0.5 * LOG2E
        for j in range(0, 3 * width, 256):
            y = mm(x, r.wqkv[:, j : j + 256])
            if j < width:
                y = y * scale
            r.qkv[rows, j : j + 256] = y.astype(bf16)

    def adapter(which, values, rows):
        source = values.astype(bf16)
        (r.src0, r.src1)[which][rows, :] = source
        before = mm_t(source, r.ad[which]) + r.adb[which : which + 1, :]
        yield
        middle, slope = gelu_and_slope(before)
        middle = middle.astype(bf16)
        (r.mid0, r.mid1)[which][rows, :] = jnp.concatenate([middle, slope.astype(bf16)], 1)
        yield
        held["up"] = mm(middle, r.au[which])
        yield

    def before_ff(batch, h):
        u = batch * per + h
        rows = rows_of(u)
        attended = mm(r.merged[rows, :], r.wo[...])
        yield
        yield from adapter(0, attended, rows)
        up = held["up"]
        sums = [0.0, 0.0]
        for b in range(blocks):
            at = rows_of(u * blocks + b, BLOCK)
            here = slice(b * BLOCK, (b + 1) * BLOCK)
            branch = attended[here] + (up[here] + r.aub[0:1, :])
            x = r.xin[at, :].astype(f32)
            valid = valid_of(batch, h, b)
            sums[0] = sums[0] + fold(x * x * valid)
            sums[1] = sums[1] + fold(branch * branch * valid)
            normal, scale = normalize(x + branch)
            r.norm0[at, :] = normal.astype(bf16)
            r.rs0[at, :] = jnp.broadcast_to(scale, (BLOCK, 128))
            normed = normal * r.gain[0:1, :] + r.shift[0:1, :]
            r.keep[local(h, b), :] = normed
            r.low[local(h, b), :] = normed.astype(bf16)
            yield
        accumulate(V_X, sums[0])
        accumulate(V_B1, sums[1])

    def ff(batch, h):
        rows = rows_of(batch * per + h)
        normed = r.low[local(h), :]
        ahead = mm(normed, r.w1[:, :256])
        act = total = None
        for j in range(0, hidden, 256):
            now = ahead
            if j + 256 < hidden:
                ahead = mm(normed, r.w1[:, j + 256 : j + 512])
            if j == 256 and h == 0:
                arrive("w2")
            if j:
                part = mm(act, r.w2[j - 256 : j, :])
                total = part if j == 256 else total + part
            act, slope = gelu_and_slope(now.astype(bf16))
            r.slope[rows, j : j + 256] = slope
            yield
        held[h] = total + mm(act, r.w2[hidden - 256 :, :])

    def after_ff(batch, h):
        u = batch * per + h
        rows = rows_of(u)
        expanded = held[h]
        yield from adapter(1, expanded, rows)
        up = held["up"]
        square = 0.0
        for b in range(blocks):
            at = rows_of(u * blocks + b, BLOCK)
            here = slice(b * BLOCK, (b + 1) * BLOCK)
            branch = expanded[here] + (up[here] + r.aub[1:2, :])
            valid = valid_of(batch, h, b)
            square = square + fold(branch * branch * valid)
            normal, scale = normalize(r.keep[local(h, b), :] + branch)
            r.norm1[at, :] = normal.astype(bf16)
            r.rs1[at, :] = jnp.broadcast_to(scale, (BLOCK, 128))
            result = ((normal * r.gain[1:2, :] + r.shift[1:2, :]) * valid).astype(bf16)
            r.xin[at, :] = result
            if hasattr(r, "send"):
                r.send[local(h, b), :] = result
            yield
        accumulate(V_B2, square)

    def adapter_back(which, rows, h):
        up = r.low[local(h), :]
        both = (r.mid0, r.mid1)[which][rows, :]
        middle, slope = both[:, :low], both[:, low:]
        before = (mm_t(up, r.au[which]) * slope.astype(f32)).astype(bf16)
        yield
        into = mm(before, r.ad[which])
        yield
        source = (r.src0, r.src1)[which][rows, :]
        flat = jnp.concatenate([middle, before], 1).T
        r.accm[(2 + which) * low : (3 + which) * low, :] += mm(flat[:low, :], up)
        r.accm[which * low : (which + 1) * low, :] += mm(flat[low:, :], source)
        yield
        accumulate(V_UP1 if which else V_UP0, fold(up.astype(f32)))
        side = jnp.zeros((UNIT, low), f32)
        wide = [side, before.astype(f32)] if which else [before.astype(f32), side]
        accumulate(V_DOWN, fold(jnp.concatenate(wide, 1)))
        held["into"] = (r.keep[local(h), :] + into).astype(bf16)
        yield

    def before_ff_back(batch, h):
        u = batch * per + h
        sums = [0.0, 0.0]
        for b in range(blocks):
            at = rows_of(u * blocks + b, BLOCK)
            grad = r.gin[local(h, b), :].astype(f32) * valid_of(batch, h, b)
            normal = r.norm1[at, :].astype(f32)
            sums[0] = sums[0] + fold(grad * normal)
            sums[1] = sums[1] + fold(grad)
            grad = normalize_back(grad, normal, spread(r.rs1[at, :], width), r.gain[1:2, :])
            r.keep[local(h, b), :] = grad
            r.low[local(h, b), :] = grad.astype(bf16)
            yield
        accumulate(V_GAIN1, sums[0])
        accumulate(V_SHIFT1, sums[1])
        yield from adapter_back(1, rows_of(u), h)
        held[h] = held["into"]

    def ff_back(batch, h):
        rows = rows_of(batch * per + h)
        down = held[h]
        ahead = mm_t(down, r.w2[:256, :])
        dhidden = total = None
        for j in range(0, hidden, 256):
            now = ahead
            if j + 256 < hidden:
                ahead = mm_t(down, r.w2[j + 256 : j + 512, :])
            if j:
                part = mm_t(dhidden, r.w1[:, j - 256 : j])
                total = part if j == 256 else total + part
            dhidden = now.astype(bf16) * r.slope[rows, j : j + 256]
            yield
        held[h] = r.keep[local(h), :] + (total + mm_t(dhidden, r.w1[:, hidden - 256 :]))

    def after_ff_back(batch, h):
        u = batch * per + h
        total = held[h]
        sums = [0.0, 0.0]
        for b in range(blocks):
            at = rows_of(u * blocks + b, BLOCK)
            grad = total[b * BLOCK : (b + 1) * BLOCK]
            normal = r.norm0[at, :].astype(f32)
            sums[0] = sums[0] + fold(grad * normal)
            sums[1] = sums[1] + fold(grad)
            grad = normalize_back(grad, normal, spread(r.rs0[at, :], width), r.gain[0:1, :])
            upper = grad.astype(bf16)
            r.norm0[at, :] = upper
            r.norm1[at, :] = (grad - upper.astype(f32)).astype(bf16)
            r.keep[local(h, b), :] = grad
            r.low[local(h, b), :] = upper
            yield
        accumulate(V_GAIN0, sums[0])
        accumulate(V_SHIFT0, sums[1])
        yield from adapter_back(0, rows_of(u), h)
        r.src0[rows_of(u), :] = held["into"]

    def to_merged(batch, h):
        rows = rows_of(batch * per + h)
        grad = r.src0[rows, :]
        parts_ = []
        for j in range(0, width, 256):
            parts_.append(mm_t(grad, r.wo[j : j + 256, :]).astype(bf16))
            yield
        r.src0[rows, :] = jnp.concatenate(parts_, 1)

    def to_input(batch, h):
        rows = rows_of(batch * per + h)
        for j in range(0, width, 256):
            part = mm_t(r.qkv[rows, :], r.wqkv[j : j + 256, :])
            part = part + r.norm0[rows, j : j + 256].astype(f32)
            r.ready[local(h), j : j + 256] = part + r.norm1[rows, j : j + 256].astype(f32)

    def forward_front(batch):
        for h in range(per):
            project(batch, h)
        long = by_batch(is_long, batch)

        @pl.when(jnp.logical_not(long))
        def _():
            for h in range(per):
                attend_short(batch * per + h)

        @pl.when(long)
        def _():
            attend_long(batch * per)

    def forward_rest(batch):
        arrive(*WEIGHTS[1:8])
        weave(before_ff(batch, 0))
        arrive("w1")
        weave(ff(batch, 0), before_ff(batch, 1))
        weave(ff(batch, 1), after_ff(batch, 0))
        weave(after_ff(batch, 1))

    def backward_rest(batch, merges):
        weave(before_ff_back(batch, 0))
        weave(ff_back(batch, 0), before_ff_back(batch, 1))
        weave(ff_back(batch, 1), after_ff_back(batch, 0))
        if merges:
            weave(after_ff_back(batch, 1), to_merged(batch, 0))
            weave(to_merged(batch, 1))
        else:
            weave(after_ff_back(batch, 1))

    def attention_back(batch, part):
        long = by_batch(is_long, batch)
        some = range(per) if part is None else (part,)

        def out(h):
            return pltpu.make_async_copy(r.ready.at[local(h)], r.grads.at[rows_of(batch * per + h)], r.sems.at[h])

        @pl.when(jnp.logical_not(long))
        def _():
            if part is not None:
                weave(to_merged(batch, part))
            for h in some:
                attend_short_back(batch * per + h)
            if part is not None:
                to_input(batch, part)
                out(part).start()
                out(part).wait()

        @pl.when(long)
        def _():
            if part == 0:
                for h in range(per):
                    weave(to_merged(batch, h))
            end = pairs // LONG_TOGETHER
            attend_long_back(batch * per, EARLY if part == 1 else 0, EARLY if part == 0 else end)
            if part != 0:
                r.qkv[rows_of(batch * per * (UNIT // TILE) + 3, TILE), :] = jnp.zeros((TILE, 3 * width), bf16)
            if part == 1:
                for h in range(per):
                    to_input(batch, h)
                    out(h).start()
                for h in range(per):
                    out(h).wait()

    if first:
        parts[0].wait()
        waits["wqkv"].wait()
        for name in WEIGHTS[1:]:
            waits[name].start()
        for copy in parts[1:]:
            copy.start()

        @pl.when(section == 0)
        def _():
            forward_front(0)
            forward_rest(0)

        @pl.when(section != 0)
        def _():
            arrive(*WEIGHTS[1:])

        for copy in parts[1:]:
            copy.wait()
    elif spec.f is not None:

        def whole_forward():
            batch = share(spec.f)

            @pl.when(section != 0)
            def _():
                r.xin[rows_of(batch, slots), :] = r.recv[...]

            forward_front(batch)
            forward_rest(batch)

        only(spec.f, whole_forward)
    if spec.a is not None:
        if spec.a[0] is not None:
            @pl.when(section == 0)
            def _():
                r.gin[...] = r.recv[...]

        only(spec.a, lambda: backward_rest(share(spec.a), spec.b is not None))

    for which, copy in copies:
        only(which, copy.wait)
    if spec.part is not None:
        only(spec.b, lambda: attention_back(share(spec.b), spec.part))
    elif spec.b is not None:
        batch_b = share(spec.b)

        def whole_back():
            attention_back(batch_b, None)
            for h in range(per):
                to_input(batch_b, h)

            r.send[...] = r.ready[...].astype(bf16)

        only(spec.b, whole_back)
    if spec.pay:
        whole = r.whole
        whole[0 : 4 * low, :] = r.accm[...]
        vectors = [jnp.sum(r.accv[8 * i : 8 * i + 8, :], 0, keepdims=True) for i in range(10)]
        total = counts[0]
        for b in range(1, batches):
            total = total + counts[b]
        vectors.append(jnp.full((1, width), total.astype(f32)))
        vectors.append(jnp.zeros((GROUP * PART_ROWS - 4 * low - len(vectors), width), f32))
        whole[4 * low :, :] = jnp.concatenate(vectors, 0)
        place = lax.axis_index("dp") % GROUP
        for o in range(GROUP):
            part = whole[rows_of(jnp.bitwise_xor(place, o), PART_ROWS), :]
            (r.part0, r.part1, r.part2, r.part3)[o][...] = part if o == 0 else part.astype(bf16)


def add_kernel(count, *refs):
    total = refs[0][...]
    for ref in refs[1 : 1 + count]:
        total = total + ref[...].astype(f32)
    refs[-2][...] = total
    refs[-1][...] = total.astype(bf16)


def finish_kernel(low, *refs):
    parts, (down, down_bias, up, up_bias, gain, shift, stats, whole) = refs[:GROUP], refs[GROUP:]
    place = lax.axis_index("dp") % GROUP
    for o in range(GROUP):
        at = pl.multiple_of(jnp.bitwise_xor(place, o) * PART_ROWS, PART_ROWS)
        whole[pl.ds(at, PART_ROWS), :] = parts[o][...].astype(f32)
    width = whole.shape[1]
    for k in range(2):
        down[k] = whole[k * low : (k + 1) * low, :]
        up[k] = whole[(2 + k) * low : (3 + k) * low, :]
    base = 4 * low
    row = lambda i: whole[base + i : base + i + 1, :]
    for out, pair in ((up_bias, (V_UP0, V_UP1)), (gain, (V_GAIN0, V_GAIN1)), (shift, (V_SHIFT0, V_SHIFT1))):
        for k in range(2):
            out[k : k + 1, :] = row(pair[k])
    for k in range(2):
        down_bias[k : k + 1, :] = row(V_DOWN)[:, k * low : (k + 1) * low]
    sums = [jnp.sum(row(i), 1, keepdims=True) for i in (V_X, V_B1, V_B2)]
    stats[...] = jnp.sqrt(jnp.concatenate(sums, 1) / (row(10)[:, :1] * width))


VSPEC = pl.BlockSpec(memory_space=pltpu.VMEM)
ASPEC = pl.BlockSpec(memory_space=pl.ANY)
SSPEC = pl.BlockSpec(memory_space=pltpu.SMEM)


def hbm(value):
    return pltpu.with_memory_space_constraint(value, pltpu.HBM)


def vmem(value):
    return pltpu.with_memory_space_constraint(value, pltpu.VMEM)


def run_step(
    env, name, first=False, f=None, a=None, b=None, part=None, before=None, done=None, cot=None, send=True, pay=False, through=None
):
    spec = SimpleNamespace(first=first, f=f, a=a, b=b, part=part, before=before, done=done, cot=cot, pay=pay)
    shapes = env.shapes
    width, hidden = shapes["w1"][0]
    sizes = (width, hidden, shapes["adb"][0][1])
    ins, in_names, in_specs = [hbm(env.seg)], ["seg"], [SSPEC]
    if first:
        for n in HELD:
            if n != "cst":
                ins.append(hbm(getattr(env, n)))
                in_names.append(n + "_hbm")
                in_specs.append(ASPEC)
    else:
        for n in HELD:
            ins.append(vmem(getattr(env, n)))
            in_names.append(n)
            in_specs.append(VSPEC)
        if cot is not None:
            ins.append(hbm(env.cot))
            in_names.append("cot")
            in_specs.append(ASPEC)
        if f is not None or a is not None:
            ins.append(vmem(env.recv))
            in_names.append("recv")
            in_specs.append(VSPEC)
    if first:
        ins.append(hbm(env.tok))
        in_names.append("tok")
        in_specs.append(ASPEC)
    outs, out_names, out_specs, alias = [], [], [], {}
    if first:
        for n in HELD:
            outs.append(pltpu.VMEM(*shapes[n]))
            out_names.append(n)
            out_specs.append(VSPEC)
    for n in STATE:
        if not first:
            alias[len(ins)] = len(outs)
            ins.append(vmem(getattr(env, n)))
            in_names.append("old_" + n)
            in_specs.append(VSPEC)
        outs.append(pltpu.VMEM(*shapes[n]))
        out_names.append(n)
        out_specs.append(VSPEC)
    for n in BIG:
        if (n == "outs" and done is None) or (n == "grads" and before is None and part is None):
            continue
        if hasattr(env, n):
            alias[len(ins)] = len(outs)
            ins.append(getattr(env, n))
            in_names.append("old_" + n)
            in_specs.append(ASPEC)
        outs.append(pltpu.HBM(*shapes[n]))
        out_names.append(n)
        out_specs.append(ASPEC)
    if through is not None:
        alias[len(ins)] = len(outs)
        ins.append(vmem(through))
        in_names.append("old_through")
        in_specs.append(VSPEC)
        outs.append(pltpu.VMEM(through.shape, through.dtype))
        out_names.append("through")
        out_specs.append(VSPEC)
    if send:
        outs.append(jax.ShapeDtypeStruct((2 * UNIT, width), bf16))
        out_names.append("send")
        out_specs.append(VSPEC)
    if pay:
        for o in range(GROUP):
            outs.append(jax.ShapeDtypeStruct((PART_ROWS, width), bf16 if o else f32))
            out_names.append("part%d" % o)
            out_specs.append(VSPEC)
    scratch = {
        "keep": pltpu.VMEM((2 * UNIT, width), f32),
        "low": pltpu.VMEM((2 * UNIT, width), bf16),
        "sems": pltpu.SemaphoreType.DMA((16,)),
    }
    if pay:
        scratch["whole"] = pltpu.VMEM((GROUP * PART_ROWS, width), f32)
    names = in_names + out_names + list(scratch)
    flops = 2 * 2 * UNIT * width * (9 * width + 2 * hidden)
    results = pl.pallas_call(
        partial(step_kernel, names, sizes, spec),
        out_shape=tuple(outs),
        in_specs=in_specs,
        out_specs=tuple(out_specs),
        scratch_shapes=list(scratch.values()),
        input_output_aliases=alias,
        compiler_params=pltpu.CompilerParams(vmem_limit_bytes=SCOPED),
        cost_estimate=pl.CostEstimate(flops=flops, bytes_accessed=2**20, transcendentals=0),
        name=name,
    )(*ins)
    vars(env).update(zip(out_names, results))


def swapped(value, axis, mask):
    count = lax.axis_size(axis)
    return lax.ppermute(value, axis, [(i, i ^ mask) for i in range(count)])


def add_up(total, terms, name):
    shape = total.shape
    return pl.pallas_call(
        partial(add_kernel, len(terms)),
        out_shape=(jax.ShapeDtypeStruct(shape, f32), jax.ShapeDtypeStruct(shape, bf16)),
        in_specs=[VSPEC] * (1 + len(terms)),
        out_specs=(VSPEC, VSPEC),
        compiler_params=pltpu.CompilerParams(vmem_limit_bytes=SCOPED),
        name=name,
    )(total, *terms)


def make_shapes(env):
    rows, width = env.tok.shape
    hidden = env.w1.shape[1]
    low = env.au.shape[1]
    shapes = {n: (getattr(env, n).shape, getattr(env, n).dtype) for n in HELD if n != "cst"}
    shapes["cst"] = ((8 * TILE, PAIR), bf16)
    wide = ((rows, width), bf16)
    for n in ("merged", "inv", "src0", "src1", "norm0", "norm1", "xin", "outs"):
        shapes[n] = wide
    shapes["qkv"] = ((rows, 3 * width), bf16)
    shapes["prob"] = ((rows * (width // PAIR), 2 * TILE), bf16)
    shapes["rs0"] = shapes["rs1"] = ((rows, 128), f32)
    shapes["slope"] = ((rows, hidden), bf16)
    shapes["mid0"] = shapes["mid1"] = ((rows, 2 * low), bf16)
    shapes["gin"] = ((2 * UNIT, width), bf16)
    shapes["ready"] = ((2 * UNIT, width), f32)
    shapes["grads"] = ((rows, width), f32)
    shapes["accm"] = ((4 * low, width), f32)
    shapes["accv"] = ((80, width), f32)
    return shapes


def local(
    tokens,
    segment_ids,
    w_qkv,
    w_attn_out,
    w_ff_in,
    w_ff_out,
    adapter_down,
    adapter_down_bias,
    adapter_up,
    adapter_up_bias,
    ln_gain,
    ln_bias,
    cotangent,
):
    batches, slots, width = tokens.shape
    low = adapter_down.shape[3]
    rows = batches * slots
    env = SimpleNamespace(
        seg=segment_ids,
        tok=tokens.reshape(rows, width),
        cot=cotangent.reshape(rows, width),
        wqkv=w_qkv[0],
        wo=w_attn_out[0],
        w1=w_ff_in[0],
        w2=w_ff_out[0],
        ad=jnp.swapaxes(adapter_down[0], 1, 2),
        au=adapter_up[0],
        adb=adapter_down_bias[0],
        aub=adapter_up_bias[0],
        gain=ln_gain[0],
        shift=ln_bias[0],
    )
    env.shapes = make_shapes(env)

    def swap():
        return lax.ppermute(env.send, "section", [(0, 1), (1, 0)])

    run_step(env, "relay0", first=True, f=(0, None))
    env.recv = swap()
    run_step(env, "relay1", f=(1, 0), done=(0, None), cot=0)
    inputs = swap()
    run_step(env, "relay2", a=(None, 0), b=(None, 0), done=(1, 0))
    gradient = swap()
    env.recv = inputs
    run_step(env, "relay3", f=(None, 1), before=(None, 0), cot=1, send=False)
    env.recv = gradient
    run_step(env, "relay4", a=(0, 1), b=(0, 1), done=(None, 1))
    env.recv = swap()
    run_step(env, "relay5", a=(1, None), before=(0, 1), send=False, pay=True)
    got = [swapped(part, "dp", o + 1) for o, part in enumerate((env.part1, env.part2, env.part3))]
    total, short = add_up(env.part0, got, "add0")
    mask = GROUP
    count = lax.axis_size("dp")
    while mask < count:
        got = swapped(short, "dp", mask)
        if 2 * mask >= count:
            run_step(env, "tail0", b=(1, None), part=0, send=False, through=total)
            total = env.through
        total, short = add_up(total, [got], "add%d" % mask)
        mask *= 2
    got = [swapped(short, "dp", o) for o in range(1, GROUP)]
    run_step(env, "tail1", b=(1, None), part=1, send=False)
    two = jax.ShapeDtypeStruct((2, width), f32)
    matrix = jax.ShapeDtypeStruct((2, low, width), f32)
    down, down_bias, up, up_bias, gain, shift, rms_stats = pl.pallas_call(
        partial(finish_kernel, low),
        out_shape=(matrix, jax.ShapeDtypeStruct((2, low), f32), matrix, two, two, two, jax.ShapeDtypeStruct((1, 3), f32)),
        in_specs=[VSPEC] * GROUP,
        out_specs=(VSPEC,) * 7,
        scratch_shapes=[pltpu.VMEM((GROUP * PART_ROWS, width), f32)],
        compiler_params=pltpu.CompilerParams(vmem_limit_bytes=SCOPED),
        name="finish",
    )(short, *got)
    return (
        env.outs.reshape(1, batches, slots, width),
        env.grads.reshape(1, batches, slots, width),
        jnp.swapaxes(down, 1, 2)[None],
        down_bias[None],
        up[None],
        up_bias[None],
        gain[None],
        shift[None],
        rms_stats,
    )


def solution(mesh):
    placed = (
        P(None, "dp", None),
        P(None, "dp"),
        P("section", None, None),
        P("section", None, None),
        P("section", None, None),
        P("section", None, None),
        P("section", None, None, None),
        P("section", None, None),
        P("section", None, None, None),
        P("section", None, None),
        P("section", None, None),
        P("section", None, None),
        P(None, "dp", None),
    )
    return jax.shard_map(
        local,
        mesh=mesh,
        in_specs=placed,
        out_specs=(
            P("section", None, "dp", None),
            P("section", None, "dp", None),
            P("section", None, None, None),
            P("section", None, None),
            P("section", None, None, None),
            P("section", None, None),
            P("section", None, None),
            P("section", None, None),
            P("section", None),
        ),
        check_vma=False,
    )
```
